32 devices in a mesh: grp: 2 (over y), tile: 4 (over z), rep: 4 (over x, core).
Axes of the slice: x: 2, y: 2, z: 4, core: 2. Of those that a mesh axis runs over, the one named last changes fastest.
Arguments:
- focusing: bfloat16 [2, 512, 1024], P(None, 'grp', 'tile'), parts along dimension 1, may hold values from -6 to 6
- source_basis: bfloat16 [2, 64, 8, 1024], P(None, 'rep', 'grp', 'tile'), parts along dimension 2, may hold values from -0.375 to 0.375
- receiver_basis: bfloat16 [2, 64, 8, 1024], P(None, 'rep', 'grp', 'tile'), parts along dimension 2, may hold values from -0.21875 to 0.21875
- tile_ranks: int32 [8, 4], P('grp', 'tile'), parts along dimension 0, may hold values from 1 to 4
- keep_counts: int32 [8], P(('grp', 'tile')), parts along dimension 0, may hold values from 64 to 256
Outputs:
- forward_data: float32 [2, 512, 1024], P(None, ('grp', 'rep'), 'tile'), parts along dimension 1
- muted_adjoint_result: float32 [2, 512, 1024], P(None, ('grp', 'rep'), 'tile'), parts along dimension 1
- correlations: float32 [2, 256, 512], P(None, 'rep', 'grp'), parts along dimension 2
The draws below stay inside these ranges and needn't reach their ends.
There are 2 independent parts, one for each index of `grp`. The reference program is written for one: setup_inputs(seed, part) draws one part's arguments, and reference() takes and returns one part's arrays. A program takes and returns all parts, laid end to end along the dimension named above; each array names one. Nothing has to cross between parts.
Inputs may be any that keep to these rules, and one draw needn't show every extreme that they name: `tile_ranks`: number of live buckets of 16 ranks in each tile. `keep_counts`: receivers kept in each receiver tile, counted from its first position.
All inputs are finite; a program needn't handle non-finite values.
Results may differ from the reference program's by a relative error of at most 0.0039.
Values may be sent and summed in bfloat16 or wider, within the bound.
A program may use at most 64 MiB of HBM per device.

```python
import math
import jax
import jax.numpy as jnp
from jax import lax

SPAN = 256
RMAX = 64
BUCKET = 16
FOC = 256
TILES = 4
NS = 1024


def touch_ends(values, own_key, low, largest):
    spot = [jax.random.randint(jax.random.fold_in(own_key, axis), (), 0, length) for axis, length in enumerate(values.shape)]
    main_axis = values.shape.index(max(values.shape))
    beside = spot[:main_axis] + [(spot[main_axis] + 1) % values.shape[main_axis]] + spot[main_axis + 1:]
    return values.at[tuple(spot)].set(low).at[tuple(beside)].set(largest)


def shard_levels(rng, shape, split, smallest, largest):
    gain = 1.0
    for position, parts in split:
        heights = jax.random.uniform(jax.random.fold_in(jax.random.fold_in(rng, 6), position), (parts,), jnp.float32, smallest / len(split), largest / len(split))
        gain = gain * jnp.repeat(jnp.exp(heights), shape[position] // parts).reshape((-1,) + (1,) * (len(shape) - 1 - position))
    return gain


def centred(key, dims, width, bound, pieces=(), held_as=jnp.bfloat16):
    result = width * jax.random.normal(key, dims, jnp.float32)
    if pieces:
        result = result * shard_levels(key, dims, pieces, -0.22, 0.18)
    return jnp.clip(result, -bound, bound).astype(held_as)


def setup_inputs(seed: int = 0, part: int = 0) -> dict:
    seeds = jax.random.split(jax.random.key(seed), 6)
    own_keys = jax.random.split(jax.random.fold_in(seeds[5], part), 6)
    focusing = centred(own_keys[0], (2, FOC, NS), 1.0, 6.0, ((2, 4),))
    source_basis = centred(own_keys[1], (2, RMAX, TILES, NS), SPAN ** -0.5, 0.375, ((1, 4), (3, 4)))
    receiver_basis = centred(own_keys[2], (2, RMAX, TILES, NS), (3 * RMAX * TILES) ** -0.5, 0.21875, ((1, 4), (3, 4)))
    tile_ranks = touch_ends(jax.random.randint(own_keys[3], (TILES, TILES), 1, RMAX // BUCKET + 1), jax.random.fold_in(own_keys[3], 1), 1, (RMAX // BUCKET + 1) - 1).astype(jnp.int32)
    keep_counts = touch_ends(jax.random.randint(own_keys[4], (TILES,), SPAN // 4, SPAN + 1), jax.random.fold_in(own_keys[4], 1), SPAN // 4, SPAN).astype(jnp.int32)
    return dict(focusing=focusing, source_basis=source_basis, receiver_basis=receiver_basis, tile_ranks=tile_ranks, keep_counts=keep_counts)


def reference(focusing, source_basis, receiver_basis, tile_ranks, keep_counts):
    bucket_index = jnp.arange(RMAX, dtype=jnp.int32) // BUCKET
    live_all = bucket_index[:, None, None] < tile_ranks[None, :, :]
    focal_wide = focusing.astype(jnp.float32)

    def forward_column(running, column):
        first_cell = (column * SPAN).astype(jnp.int32)
        basis_column_vector = lax.dynamic_slice_in_dim(source_basis, first_cell, SPAN, 3).astype(jnp.float32)
        focal_col = lax.dynamic_slice_in_dim(focal_wide, first_cell, SPAN, 2)
        blocks = jnp.einsum('pkas,qfs->pqkaf', basis_column_vector, focal_col)
        live_col = lax.dynamic_index_in_dim(live_all, column, 2, keepdims=False)
        stacked = jnp.stack([blocks[0, 0] - blocks[1, 1], blocks[0, 1] + blocks[1, 0]])
        rounded = jnp.where(live_col[None, :, :, None], stacked, 0.0).astype(jnp.bfloat16)
        coefficient = lax.optimization_barrier(rounded).astype(jnp.float32)
        lifting = lax.dynamic_index_in_dim(receiver_basis, column, 2, keepdims=False)
        lifting = lifting.astype(jnp.float32).reshape(2, RMAX, TILES, SPAN)
        blocks = jnp.einsum('pkaf,qkar->pqfar', coefficient, lifting)
        return (running + jnp.stack([blocks[0, 0] - blocks[1, 1], blocks[1, 0] + blocks[0, 1]]), None)
    columns_all = jnp.arange(TILES, dtype=jnp.int32)
    start_value = jnp.zeros((2, FOC, TILES, SPAN), jnp.float32)
    forward_grid, unused = lax.scan(forward_column, start_value, columns_all)
    forward_data = forward_grid.reshape(2, FOC, NS)
    weights = (jnp.arange(SPAN, dtype=jnp.int32)[None, :] < keep_counts[:, None]).astype(jnp.float32).reshape(NS)
    masked = (forward_data * weights).astype(jnp.bfloat16)
    masked_wide = lax.optimization_barrier(masked).astype(jnp.float32).reshape(2, FOC, TILES, SPAN)

    def adjoint_column(running, column):
        first_cell = (column * SPAN).astype(jnp.int32)
        lifting = lax.dynamic_index_in_dim(receiver_basis, column, 2, keepdims=False)
        lifting = lifting.astype(jnp.float32).reshape(2, RMAX, TILES, SPAN)
        blocks = jnp.einsum('pkar,qfar->pqkaf', lifting, masked_wide)
        stacked = jnp.stack([blocks[0, 0] + blocks[1, 1], blocks[0, 1] - blocks[1, 0]])
        live_col = lax.dynamic_index_in_dim(live_all, column, 2, keepdims=False)
        rounded = jnp.where(live_col[None, :, :, None], stacked, 0.0).astype(jnp.bfloat16)
        coefficient = lax.optimization_barrier(rounded).astype(jnp.float32)
        basis_column_vector = lax.dynamic_slice_in_dim(source_basis, first_cell, SPAN, 3).astype(jnp.float32)
        blocks = jnp.einsum('pkaf,qkas->pqfs', coefficient, basis_column_vector)
        return (running, jnp.stack([blocks[0, 0] + blocks[1, 1], blocks[1, 0] - blocks[0, 1]]))
    unused_two, image_cols = lax.scan(adjoint_column, jnp.zeros((), jnp.float32), columns_all)
    muted_adjoint_result = jnp.transpose(image_cols, (1, 2, 0, 3)).reshape(2, FOC, NS)
    blocks = jnp.einsum('pgs,qfs->pqgf', muted_adjoint_result, focal_wide, precision=lax.Precision.HIGHEST)
    factor = 1.0 / math.sqrt(SPAN * NS)
    correlations = factor * jnp.stack([blocks[0, 0] + blocks[1, 1], blocks[1, 0] - blocks[0, 1]])
    return (forward_data, muted_adjoint_result, correlations)
```

```python
import functools
import math

import jax
import jax.numpy as jnp
from jax import lax
from jax.experimental import pallas as pl
from jax.experimental.pallas import tpu as pltpu
from jax.sharding import PartitionSpec as P

SPAN = 256
BUCKET = 16
FOC = 256
MESH = pl.DeviceIdType.MESH

NT = (((1,), (1,)), ((), ()))
TN = (((0,), (0,)), ((), ()))


def dot(a, b, dims):
    return lax.dot_general(a, b, dims, preferred_element_type=jnp.float32)


def each(first, last, body):
    if last - first <= 16:
        for i in range(first, last):
            body(i)
    else:
        pl.loop(first, last)(body)


def kernel(tiles, reps, reduce_here, factor, foc_ref, sb_ref, rb_ref, keep_ref,
           fwd_ref, mar_ref, cor_ref,
           rb_all, sb_all, coef_out, coef_in, back_out, back_in, red_out, red_in, cor_all,
           coef_send, coef_recv, rb_send, rb_recv, sb_send, sb_recv,
           back_send, back_recv, red_send, red_recv, cor_send, cor_recv):
    t = lax.axis_index("tile")
    r = lax.axis_index("rep")
    me = t * reps + r
    count = tiles * reps
    ranks, span = sb_ref.shape[2], sb_ref.shape[3]
    share = foc_ref.shape[1] // reps
    rows = reps * tiles * ranks

    def peer(d):
        other = lax.rem(me + d, count)
        return other // reps, lax.rem(other, reps)

    barrier = pltpu.get_barrier_semaphore()

    def greet(d):
        pt, pr = peer(d)
        pl.semaphore_signal(barrier, inc=1, device_id={"tile": pt, "rep": pr}, device_id_type=MESH)

    each(1, count, greet)

    shares, turned = [], []
    for j in range(reps):
        re = foc_ref[0, j * share:(j + 1) * share, :]
        im = foc_ref[1, j * share:(j + 1) * share, :]
        shares += [re, im]
        turned += [-im, re]
    coef = dot(sb_ref[0].reshape(tiles * ranks, span), jnp.concatenate(shares, 0), NT)
    coef += dot(sb_ref[1].reshape(tiles * ranks, span), jnp.concatenate(turned, 0), NT)
    coef = coef.astype(jnp.bfloat16).reshape(tiles, ranks, reps * 2 * share)
    for j in range(reps):
        coef_out[j] = coef[:, :, j * 2 * share:(j + 1) * 2 * share]

    pl.semaphore_wait(barrier, count - 1)

    def basis_copy(src, dst, send, recv, d):
        return pltpu.make_async_remote_copy(
            src_ref=src, dst_ref=dst.at[r], send_sem=send.at[d], recv_sem=recv.at[d],
            device_id={"tile": t, "rep": lax.rem(r + d, reps)}, device_id_type=MESH)

    def coef_copy(d):
        pt, pr = peer(d)
        return pltpu.make_async_remote_copy(
            src_ref=coef_out.at[pr, pt], dst_ref=coef_in.at[r, t],
            send_sem=coef_send.at[d], recv_sem=coef_recv.at[d],
            device_id={"tile": pt, "rep": pr}, device_id_type=MESH)

    def tile_copy(src, dst, send, recv, d):
        return pltpu.make_async_remote_copy(
            src_ref=src, dst_ref=dst, send_sem=send.at[d], recv_sem=recv.at[d],
            device_id={"tile": lax.rem(t + d, tiles), "rep": r}, device_id_type=MESH)

    rb_copies = [basis_copy(rb_ref, rb_all, rb_send, rb_recv, d) for d in range(1, reps)]
    sb_copies = [basis_copy(sb_ref, sb_all, sb_send, sb_recv, d) for d in range(1, reps)]
    each(1, count, lambda d: coef_copy(d).start())
    for c in rb_copies:
        c.start()
    for c in sb_copies:
        c.start()
    rb_all[r] = rb_ref[...]
    sb_all[r] = sb_ref[...]
    coef_in[r, t] = coef_out[r, t]

    for c in rb_copies:
        c.wait_recv()
    each(1, count, lambda d: coef_copy(d).wait_recv())

    arrived = coef_in[...].reshape(rows, 2 * share)
    rre = rb_all[:, 0].reshape(rows, span)
    rim = rb_all[:, 1].reshape(rows, span)
    g0 = dot(arrived, rre, TN)
    g1 = dot(arrived, rim, TN)
    fre = g0[:share] - g1[share:]
    fim = g0[share:] + g1[:share]
    fwd_ref[0] = fre
    fwd_ref[1] = fim
    kept = lax.broadcasted_iota(jnp.int32, (share, span), 1) < keep_ref[0]
    mre = jnp.where(kept, fre, 0.0).astype(jnp.bfloat16)
    mim = jnp.where(kept, fim, 0.0).astype(jnp.bfloat16)
    back = dot(rre, jnp.concatenate([mre, mim], 0), NT)
    back += dot(rim, jnp.concatenate([mim, -mre], 0), NT)
    back_out[...] = back.astype(jnp.bfloat16).reshape(reps, tiles, ranks, 2 * share)

    def back_copy(d):
        return tile_copy(back_out.at[:, lax.rem(t + d, tiles)], back_in.at[:, t], back_send, back_recv, d)

    each(1, tiles, lambda d: back_copy(d).start())
    back_in[:, t] = back_out[:, t]
    for c in sb_copies:
        c.wait_recv()
    each(1, tiles, lambda d: back_copy(d).wait_recv())

    arrived = back_in[...].reshape(rows, 2 * share)
    h0 = dot(arrived, sb_all[:, 0].reshape(rows, span), TN)
    h1 = dot(arrived, sb_all[:, 1].reshape(rows, span), TN)
    are = h0[:share] + h1[share:]
    aim = h0[share:] - h1[:share]
    mar_ref[0] = are
    mar_ref[1] = aim

    are = are.astype(jnp.bfloat16)
    aim = aim.astype(jnp.bfloat16)
    part_re = dot(are, foc_ref[0], NT) + dot(aim, foc_ref[1], NT)
    part_im = dot(aim, foc_ref[0], NT) - dot(are, foc_ref[1], NT)
    if reduce_here:
        part = jnp.concatenate([part_re, part_im], 0).astype(jnp.bfloat16)
        red_out[...] = part.reshape(red_out.shape)

        def red_copy(d):
            return tile_copy(red_out.at[lax.rem(t + d, tiles)], red_in.at[t], red_send, red_recv, d)

        def cor_copy(d):
            return tile_copy(cor_all.at[t], cor_all.at[t], cor_send, cor_recv, d)

        each(1, tiles, lambda d: red_copy(d).start())
        red_in[t] = red_out[t]
        each(1, tiles, lambda d: red_copy(d).wait_recv())
        total = red_in[0].astype(jnp.float32)
        for j in range(1, tiles):
            total += red_in[j].astype(jnp.float32)
        cor_all[t] = (factor * total).astype(jnp.bfloat16)
        each(1, tiles, lambda d: cor_copy(d).start())
        each(1, tiles, lambda d: cor_copy(d).wait_recv())
        cor_ref[...] = cor_all[...].astype(jnp.float32).reshape(cor_ref.shape)
        each(1, tiles, lambda d: red_copy(d).wait_send())
        each(1, tiles, lambda d: cor_copy(d).wait_send())
    else:
        cor_ref[0] = factor * part_re
        cor_ref[1] = factor * part_im

    each(1, count, lambda d: coef_copy(d).wait_send())
    for c in rb_copies + sb_copies:
        c.wait_send()
    each(1, tiles, lambda d: back_copy(d).wait_send())


def per_device(focusing, source_basis, receiver_basis, tile_ranks, keep_counts):
    tiles, reps = lax.axis_size("tile"), lax.axis_size("rep")
    _, ranks, _, span = source_basis.shape
    points = focusing.shape[1]
    share = points // reps
    factor = 1.0 / math.sqrt(SPAN * span * tiles)
    first = lax.axis_index("rep") * ranks
    live = (first + lax.iota(jnp.int32, ranks))[:, None] // BUCKET < tile_ranks[:, 0][None, :]
    sb = jnp.where(live[None, :, :, None], source_basis, jnp.zeros((), jnp.bfloat16))
    sb = jnp.transpose(sb, (0, 2, 1, 3))
    rb = jnp.transpose(receiver_basis, (0, 2, 1, 3))
    reduce_here = (2 * share) % (16 * tiles) == 0
    chunk = 2 * share // tiles if reduce_here else 16
    bf = jnp.bfloat16
    dma = pltpu.SemaphoreType.DMA
    vmem = pl.BlockSpec(memory_space=pltpu.VMEM)
    fwd, mar, cor = pl.pallas_call(
        functools.partial(kernel, tiles, reps, reduce_here, factor),
        out_shape=(
            jax.ShapeDtypeStruct((2, share, span), jnp.float32),
            jax.ShapeDtypeStruct((2, share, span), jnp.float32),
            jax.ShapeDtypeStruct((2, share, points), jnp.float32),
        ),
        in_specs=[vmem, vmem, vmem, pl.BlockSpec(memory_space=pltpu.SMEM)],
        out_specs=(vmem, vmem, vmem),
        scratch_shapes=[
            pltpu.VMEM((reps, 2, tiles, ranks, span), bf),
            pltpu.VMEM((reps, 2, tiles, ranks, span), bf),
            pltpu.VMEM((reps, tiles, ranks, 2 * share), bf),
            pltpu.VMEM((reps, tiles, ranks, 2 * share), bf),
            pltpu.VMEM((reps, tiles, ranks, 2 * share), bf),
            pltpu.VMEM((reps, tiles, ranks, 2 * share), bf),
            pltpu.VMEM((tiles, chunk, points), bf),
            pltpu.VMEM((tiles, chunk, points), bf),
            pltpu.VMEM((tiles, chunk, points), bf),
            dma((tiles * reps,)), dma((tiles * reps,)),
            dma((reps,)), dma((reps,)), dma((reps,)), dma((reps,)),
            dma((tiles,)), dma((tiles,)), dma((tiles,)), dma((tiles,)), dma((tiles,)), dma((tiles,)),
        ],
        compiler_params=pltpu.CompilerParams(
            collective_id=0, has_side_effects=True, vmem_limit_bytes=56 * 2 ** 20),
    )(focusing, sb, rb, keep_counts)
    if not reduce_here:
        cor = lax.psum(cor, "tile")
    return fwd, mar, cor


def solution(mesh):
    placed = (
        P(None, "grp", "tile"),
        P(None, "rep", "grp", "tile"),
        P(None, "rep", "grp", "tile"),
        P("grp", "tile"),
        P(("grp", "tile")),
    )
    return jax.shard_map(
        per_device,
        mesh=mesh,
        in_specs=placed,
        out_specs=(
            P(None, ("grp", "rep"), "tile"),
            P(None, ("grp", "rep"), "tile"),
            P(None, "rep", "grp"),
        ),
        check_vma=False,
    )
```

```python
import functools
import math

import jax
import jax.numpy as jnp
from jax import lax
from jax.experimental import pallas as pl
from jax.experimental.pallas import tpu as pltpu
from jax.sharding import PartitionSpec as P

SPAN = 256
BUCKET = 16
FOC = 256
MESH = pl.DeviceIdType.MESH

NT = (((1,), (1,)), ((), ()))
TN = (((0,), (0,)), ((), ()))


def dot(a, b, dims):
    return lax.dot_general(a, b, dims, preferred_element_type=jnp.float32)


def each(first, last, body):
    if last - first <= 16:
        for i in range(first, last):
            body(i)
    else:
        pl.loop(first, last)(body)


def kernel(tiles, reps, reduce_here, factor, foc_ref, source_ref, receiver_ref, ranks_ref, keep_ref,
           fwd_ref, mar_ref, cor_ref,
           sb_ref, rb_ref, rb_all, sb_all, coef_out, coef_in, back_out, back_in, red_out, red_in, cor_all,
           coef_send, coef_recv, rb_send, rb_recv, sb_send, sb_recv,
           back_send, back_recv, red_send, red_recv, cor_send, cor_recv):
    t = lax.axis_index("tile")
    r = lax.axis_index("rep")
    me = t * reps + r
    count = tiles * reps
    ranks, span = sb_ref.shape[2], sb_ref.shape[3]
    share = foc_ref.shape[1] // reps
    rows = reps * tiles * ranks

    def peer(d):
        other = lax.rem(me + d, count)
        return other // reps, lax.rem(other, reps)

    barrier = pltpu.get_barrier_semaphore()

    def greet(d):
        pt, pr = peer(d)
        pl.semaphore_signal(barrier, inc=1, device_id={"tile": pt, "rep": pr}, device_id_type=MESH)

    each(1, count, greet)

    bucket = (r * ranks + lax.broadcasted_iota(jnp.int32, (2, ranks, span), 1)) // BUCKET
    for a in range(tiles):
        wide = source_ref[:, :, a, :].astype(jnp.float32)
        sb_ref[:, a] = jnp.where(bucket < ranks_ref[a], wide, 0.0).astype(jnp.bfloat16)
        rb_ref[:, a] = receiver_ref[:, :, a, :]

    shares, turned = [], []
    for j in range(reps):
        re = foc_ref[0, j * share:(j + 1) * share, :]
        im = foc_ref[1, j * share:(j + 1) * share, :]
        shares += [re, im]
        turned += [-im, re]
    coef = dot(sb_ref[0].reshape(tiles * ranks, span), jnp.concatenate(shares, 0), NT)
    coef += dot(sb_ref[1].reshape(tiles * ranks, span), jnp.concatenate(turned, 0), NT)
    coef = coef.astype(jnp.bfloat16).reshape(tiles, ranks, reps * 2 * share)
    for j in range(reps):
        coef_out[j] = coef[:, :, j * 2 * share:(j + 1) * 2 * share]

    pl.semaphore_wait(barrier, count - 1)

    class Gather:
        def __init__(self, own, held, send, recv):
            self.own, self.held, self.send, self.recv = own, held, send, recv
            if reps == 4:
                self.first = [self.copy(own, r, r ^ 2, 0), self.copy(own, r, r ^ 1, 1)]
                self.second = [self.copy(held.at[r ^ 2], r ^ 2, r ^ 1, 2)]
            else:
                self.first = [self.copy(own, r, lax.rem(r + d, reps), d - 1) for d in range(1, reps)]
                self.second = []

        def copy(self, src, slot, to, i):
            return pltpu.make_async_remote_copy(
                src_ref=src, dst_ref=self.held.at[slot], send_sem=self.send.at[i], recv_sem=self.recv.at[i],
                device_id={"tile": t, "rep": to}, device_id_type=MESH)

        def start(self):
            for c in self.first:
                c.start()
            self.held[r] = self.own[...]

        def forward(self):
            if self.second:
                self.first[0].wait_recv()
                self.second[0].start()

        def wait_recv(self):
            for c in (self.first[1:] if self.second else self.first) + self.second:
                c.wait_recv()

        def wait_send(self):
            for c in self.first + self.second:
                c.wait_send()

    def coef_copy(d):
        pt, pr = peer(d)
        return pltpu.make_async_remote_copy(
            src_ref=coef_out.at[pr, pt], dst_ref=coef_in.at[r, t],
            send_sem=coef_send.at[d], recv_sem=coef_recv.at[d],
            device_id={"tile": pt, "rep": pr}, device_id_type=MESH)

    def tile_copy(src, dst, send, recv, d):
        return pltpu.make_async_remote_copy(
            src_ref=src, dst_ref=dst, send_sem=send.at[d], recv_sem=recv.at[d],
            device_id={"tile": lax.rem(t + d, tiles), "rep": r}, device_id_type=MESH)

    rb_gather = Gather(rb_ref, rb_all, rb_send, rb_recv)
    sb_gather = Gather(sb_ref, sb_all, sb_send, sb_recv)
    rb_gather.start()
    each(1, count, lambda d: coef_copy(d).start())
    sb_gather.start()
    coef_in[r, t] = coef_out[r, t]

    rb_gather.forward()
    rb_gather.wait_recv()
    each(1, count, lambda d: coef_copy(d).wait_recv())

    sb_gather.forward()

    arrived = coef_in[...].reshape(rows, 2 * share)
    rre = rb_all[:, 0].reshape(rows, span)
    rim = rb_all[:, 1].reshape(rows, span)
    g0 = dot(arrived, rre, TN)
    g1 = dot(arrived, rim, TN)
    fre = g0[:share] - g1[share:]
    fim = g0[share:] + g1[:share]
    fwd_ref[0] = fre
    fwd_ref[1] = fim
    kept = lax.broadcasted_iota(jnp.int32, (share, span), 1) < keep_ref[0]
    mre = jnp.where(kept, fre, 0.0).astype(jnp.bfloat16)
    mim = jnp.where(kept, fim, 0.0).astype(jnp.bfloat16)
    back = dot(rre, jnp.concatenate([mre, mim], 0), NT)
    back += dot(rim, jnp.concatenate([mim, -mre], 0), NT)
    back_out[...] = back.astype(jnp.bfloat16).reshape(reps, tiles, ranks, 2 * share)

    def back_copy(d):
        return tile_copy(back_out.at[:, lax.rem(t + d, tiles)], back_in.at[:, t], back_send, back_recv, d)

    each(1, tiles, lambda d: back_copy(d).start())
    back_in[:, t] = back_out[:, t]
    sb_gather.wait_recv()
    each(1, tiles, lambda d: back_copy(d).wait_recv())

    arrived = back_in[...].reshape(rows, 2 * share)
    h0 = dot(arrived, sb_all[:, 0].reshape(rows, span), TN)
    h1 = dot(arrived, sb_all[:, 1].reshape(rows, span), TN)
    are = h0[:share] + h1[share:]
    aim = h0[share:] - h1[:share]
    mar_ref[0] = are
    mar_ref[1] = aim

    are = are.astype(jnp.bfloat16)
    aim = aim.astype(jnp.bfloat16)
    part_re = dot(are, foc_ref[0], NT) + dot(aim, foc_ref[1], NT)
    part_im = dot(aim, foc_ref[0], NT) - dot(are, foc_ref[1], NT)
    if reduce_here:
        part = jnp.concatenate([part_re, part_im], 0).astype(jnp.bfloat16)
        red_out[...] = part.reshape(red_out.shape)

        def red_copy(d):
            return tile_copy(red_out.at[lax.rem(t + d, tiles)], red_in.at[t], red_send, red_recv, d)

        def cor_copy(d):
            return tile_copy(cor_all.at[t], cor_all.at[t], cor_send, cor_recv, d)

        each(1, tiles, lambda d: red_copy(d).start())
        red_in[t] = red_out[t]
        each(1, tiles, lambda d: red_copy(d).wait_recv())
        total = red_in[0].astype(jnp.float32)
        for j in range(1, tiles):
            total += red_in[j].astype(jnp.float32)
        cor_all[t] = (factor * total).astype(jnp.bfloat16)
        each(1, tiles, lambda d: cor_copy(d).start())
        each(1, tiles, lambda d: cor_copy(d).wait_recv())
        cor_ref[...] = cor_all[...].astype(jnp.float32).reshape(cor_ref.shape)
        each(1, tiles, lambda d: red_copy(d).wait_send())
        each(1, tiles, lambda d: cor_copy(d).wait_send())
    else:
        cor_ref[0] = factor * part_re
        cor_ref[1] = factor * part_im

    each(1, count, lambda d: coef_copy(d).wait_send())
    rb_gather.wait_send()
    sb_gather.wait_send()
    each(1, tiles, lambda d: back_copy(d).wait_send())


def per_device(focusing, source_basis, receiver_basis, tile_ranks, keep_counts):
    tiles, reps = lax.axis_size("tile"), lax.axis_size("rep")
    _, ranks, _, span = source_basis.shape
    points = focusing.shape[1]
    share = points // reps
    factor = 1.0 / math.sqrt(SPAN * span * tiles)
    reduce_here = (2 * share) % (16 * tiles) == 0
    chunk = 2 * share // tiles if reduce_here else 16
    bf = jnp.bfloat16
    dma = pltpu.SemaphoreType.DMA
    smem = pl.BlockSpec(memory_space=pltpu.SMEM)
    vmem = pl.BlockSpec(memory_space=pltpu.VMEM)
    fwd, mar, cor = pl.pallas_call(
        functools.partial(kernel, tiles, reps, reduce_here, factor),
        out_shape=(
            jax.ShapeDtypeStruct((2, share, span), jnp.float32),
            jax.ShapeDtypeStruct((2, share, span), jnp.float32),
            jax.ShapeDtypeStruct((2, share, points), jnp.float32),
        ),
        in_specs=[vmem, vmem, vmem, smem, smem],
        out_specs=(vmem, vmem, vmem),
        scratch_shapes=[
            pltpu.VMEM((2, tiles, ranks, span), bf),
            pltpu.VMEM((2, tiles, ranks, span), bf),
            pltpu.VMEM((reps, 2, tiles, ranks, span), bf),
            pltpu.VMEM((reps, 2, tiles, ranks, span), bf),
            pltpu.VMEM((reps, tiles, ranks, 2 * share), bf),
            pltpu.VMEM((reps, tiles, ranks, 2 * share), bf),
            pltpu.VMEM((reps, tiles, ranks, 2 * share), bf),
            pltpu.VMEM((reps, tiles, ranks, 2 * share), bf),
            pltpu.VMEM((tiles, chunk, points), bf),
            pltpu.VMEM((tiles, chunk, points), bf),
            pltpu.VMEM((tiles, chunk, points), bf),
            dma((tiles * reps,)), dma((tiles * reps,)),
            dma((reps,)), dma((reps,)), dma((reps,)), dma((reps,)),
            dma((tiles,)), dma((tiles,)), dma((tiles,)), dma((tiles,)), dma((tiles,)), dma((tiles,)),
        ],
        compiler_params=pltpu.CompilerParams(
            collective_id=0, has_side_effects=True, vmem_limit_bytes=56 * 2 ** 20),
    )(focusing, source_basis, receiver_basis, tile_ranks.reshape(tiles), keep_counts)
    if not reduce_here:
        cor = lax.psum(cor, "tile")
    return fwd, mar, cor


def solution(mesh):
    placed = (
        P(None, "grp", "tile"),
        P(None, "rep", "grp", "tile"),
        P(None, "rep", "grp", "tile"),
        P("grp", "tile"),
        P(("grp", "tile")),
    )
    return jax.shard_map(
        per_device,
        mesh=mesh,
        in_specs=placed,
        out_specs=(
            P(None, ("grp", "rep"), "tile"),
            P(None, ("grp", "rep"), "tile"),
            P(None, "rep", "grp"),
        ),
        check_vma=False,
    )
```

```python
import functools
import math

import jax
import jax.numpy as jnp
from jax import lax
from jax.experimental import pallas as pl
from jax.experimental.pallas import tpu as pltpu
from jax.sharding import PartitionSpec as P

SPAN = 256
BUCKET = 16
FOC = 256
MESH = pl.DeviceIdType.MESH

NT = (((1,), (1,)), ((), ()))
TN = (((0,), (0,)), ((), ()))


def dot(a, b, dims):
    return lax.dot_general(a, b, dims, preferred_element_type=jnp.float32)


def each(first, last, body):
    if last - first <= 16:
        for i in range(first, last):
            body(i)
    else:
        pl.loop(first, last)(body)


def kernel(tiles, reps, reduce_here, factor, foc_ref, source_ref, receiver_ref, ranks_ref, keep_ref,
           fwd_ref, mar_ref, cor_ref,
           sb_ref, rb_ref, rb_all, sb_all, coef_out, coef_in, back_out, back_in, red_out, red_in, cor_all,
           near_out, near_in, near_all,
           near_send, near_recv, row_send, row_recv,
           coef_send, coef_recv, rb_send, rb_recv, sb_send, sb_recv,
           back_send, back_recv, red_send, red_recv, cor_send, cor_recv):
    t = lax.axis_index("tile")
    r = lax.axis_index("rep")
    me = t * reps + r
    count = tiles * reps
    ranks, span = sb_ref.shape[2], sb_ref.shape[3]
    share = foc_ref.shape[1] // reps
    rows = reps * tiles * ranks

    def peer(d):
        other = lax.rem(me + d, count)
        return other // reps, lax.rem(other, reps)

    barrier = pltpu.get_barrier_semaphore()

    def greet(d):
        pt, pr = peer(d)
        pl.semaphore_signal(barrier, inc=1, device_id={"tile": pt, "rep": pr}, device_id_type=MESH)

    each(1, count, greet)

    bucket = (r * ranks + lax.broadcasted_iota(jnp.int32, (2, ranks, span), 1)) // BUCKET
    for a in range(tiles):
        wide = source_ref[:, :, a, :].astype(jnp.float32)
        sb_ref[:, a] = jnp.where(bucket < ranks_ref[a], wide, 0.0).astype(jnp.bfloat16)
        rb_ref[:, a] = receiver_ref[:, :, a, :]

    shares, turned = [], []
    for j in range(reps):
        re = foc_ref[0, j * share:(j + 1) * share, :]
        im = foc_ref[1, j * share:(j + 1) * share, :]
        shares += [re, im]
        turned += [-im, re]
    coef = dot(sb_ref[0].reshape(tiles * ranks, span), jnp.concatenate(shares, 0), NT)
    coef += dot(sb_ref[1].reshape(tiles * ranks, span), jnp.concatenate(turned, 0), NT)
    coef = coef.astype(jnp.bfloat16).reshape(tiles, ranks, reps * 2 * share)
    for j in range(reps):
        coef_out[j] = coef[:, :, j * 2 * share:(j + 1) * 2 * share]

    pl.semaphore_wait(barrier, count - 1)

    class Gather:
        def __init__(self, own, held, send, recv):
            self.own, self.held, self.send, self.recv = own, held, send, recv
            if reps == 4:
                self.first = [self.copy(own, r, r ^ 2, 0), self.copy(own, r, r ^ 1, 1)]
                self.second = [self.copy(held.at[r ^ 2], r ^ 2, r ^ 1, 2)]
            else:
                self.first = [self.copy(own, r, lax.rem(r + d, reps), d - 1) for d in range(1, reps)]
                self.second = []

        def copy(self, src, slot, to, i):
            return pltpu.make_async_remote_copy(
                src_ref=src, dst_ref=self.held.at[slot], send_sem=self.send.at[i], recv_sem=self.recv.at[i],
                device_id={"tile": t, "rep": to}, device_id_type=MESH)

        def start(self):
            for c in self.first:
                c.start()
            self.held[r] = self.own[...]

        def forward(self):
            if self.second:
                self.first[0].wait_recv()
                self.second[0].start()

        def wait_recv(self):
            for c in (self.first[1:] if self.second else self.first) + self.second:
                c.wait_recv()

        def wait_send(self):
            for c in self.first + self.second:
                c.wait_send()

    def coef_copy(d):
        pt, pr = peer(d)
        return pltpu.make_async_remote_copy(
            src_ref=coef_out.at[pr, pt], dst_ref=coef_in.at[r, t],
            send_sem=coef_send.at[d], recv_sem=coef_recv.at[d],
            device_id={"tile": pt, "rep": pr}, device_id_type=MESH)

    def tile_copy(src, dst, send, recv, d):
        return pltpu.make_async_remote_copy(
            src_ref=src, dst_ref=dst, send_sem=send.at[d], recv_sem=recv.at[d],
            device_id={"tile": lax.rem(t + d, tiles), "rep": r}, device_id_type=MESH)

    def near_copy(d):
        return tile_copy(near_out.at[lax.rem(t + d, tiles)], near_in.at[t], near_send, near_recv, d)

    rb_gather = Gather(rb_ref, rb_all, rb_send, rb_recv)
    sb_gather = Gather(sb_ref, sb_all, sb_send, sb_recv)
    row_gather = Gather(near_in, near_all, row_send, row_recv)
    rb_gather.start()
    each(1, count, lambda d: coef_copy(d).start())
    coef_in[r, t] = coef_out[r, t]
    if reduce_here:
        fre, fim = foc_ref[0], foc_ref[1]
        coef = dot(sb_ref[0].reshape(tiles * ranks, span), jnp.concatenate([fre, fim], 0), NT)
        coef += dot(sb_ref[1].reshape(tiles * ranks, span), jnp.concatenate([-fim, fre], 0), NT)
        near_out[...] = coef.astype(jnp.bfloat16).reshape(near_out.shape)
        each(1, tiles, lambda d: near_copy(d).start())
        near_in[t] = near_out[t]
    sb_gather.start()

    rb_gather.forward()
    if reduce_here:
        each(1, tiles, lambda d: near_copy(d).wait_recv())
        row_gather.start()
    rb_gather.wait_recv()
    each(1, count, lambda d: coef_copy(d).wait_recv())

    arrived = coef_in[...].reshape(rows, 2 * share)
    rre = rb_all[:, 0].reshape(rows, span)
    rim = rb_all[:, 1].reshape(rows, span)
    g0 = dot(arrived, rre, TN)
    g1 = dot(arrived, rim, TN)
    fre = g0[:share] - g1[share:]
    fim = g0[share:] + g1[:share]
    fwd_ref[0] = fre
    fwd_ref[1] = fim
    if reduce_here:
        row_gather.forward()
    kept = lax.broadcasted_iota(jnp.int32, (share, span), 1) < keep_ref[0]
    mre = jnp.where(kept, fre, 0.0).astype(jnp.bfloat16)
    mim = jnp.where(kept, fim, 0.0).astype(jnp.bfloat16)
    back = dot(rre, jnp.concatenate([mre, mim], 0), NT)
    back += dot(rim, jnp.concatenate([mim, -mre], 0), NT)
    back = back.astype(jnp.bfloat16)
    back_out[...] = back.reshape(reps, tiles, ranks, 2 * share)

    def back_copy(d):
        return tile_copy(back_out.at[:, lax.rem(t + d, tiles)], back_in.at[:, t], back_send, back_recv, d)

    def red_copy(d):
        return tile_copy(red_out.at[lax.rem(t + d, tiles)], red_in.at[t], red_send, red_recv, d)

    def cor_copy(d):
        return tile_copy(cor_all.at[t], cor_all.at[t], cor_send, cor_recv, d)

    each(1, tiles, lambda d: back_copy(d).start())
    back_in[:, t] = back_out[:, t]

    if reduce_here:
        row_gather.wait_recv()
        both = dot(back, near_all[...].reshape(rows, 2 * reps * share), TN)
        points = reps * share
        part_re = both[:share, :points] + both[share:, points:]
        part_im = both[share:, :points] - both[:share, points:]
        part = jnp.concatenate([part_re, part_im], 0).astype(jnp.bfloat16)
        red_out[...] = part.reshape(red_out.shape)
        each(1, tiles, lambda d: red_copy(d).start())
        red_in[t] = red_out[t]

    sb_gather.forward()
    each(1, tiles, lambda d: back_copy(d).wait_recv())
    if reduce_here:
        each(1, tiles, lambda d: red_copy(d).wait_recv())
        total = red_in[0].astype(jnp.float32)
        for j in range(1, tiles):
            total += red_in[j].astype(jnp.float32)
        cor_all[t] = (factor * total).astype(jnp.bfloat16)
        each(1, tiles, lambda d: cor_copy(d).start())

    sb_gather.wait_recv()
    arrived = back_in[...].reshape(rows, 2 * share)
    h0 = dot(arrived, sb_all[:, 0].reshape(rows, span), TN)
    h1 = dot(arrived, sb_all[:, 1].reshape(rows, span), TN)
    are = h0[:share] + h1[share:]
    aim = h0[share:] - h1[:share]
    mar_ref[0] = are
    mar_ref[1] = aim

    if reduce_here:
        each(1, count, lambda d: coef_copy(d).wait_send())
        each(1, tiles, lambda d: near_copy(d).wait_send())
        each(1, tiles, lambda d: red_copy(d).wait_send())
        row_gather.wait_send()
        each(1, tiles, lambda d: cor_copy(d).wait_recv())
        cor_ref[...] = cor_all[...].astype(jnp.float32).reshape(cor_ref.shape)
        each(1, tiles, lambda d: cor_copy(d).wait_send())
    else:
        are = are.astype(jnp.bfloat16)
        aim = aim.astype(jnp.bfloat16)
        cor_ref[0] = factor * (dot(are, foc_ref[0], NT) + dot(aim, foc_ref[1], NT))
        cor_ref[1] = factor * (dot(aim, foc_ref[0], NT) - dot(are, foc_ref[1], NT))
        each(1, count, lambda d: coef_copy(d).wait_send())
    rb_gather.wait_send()
    sb_gather.wait_send()
    each(1, tiles, lambda d: back_copy(d).wait_send())


def per_device(focusing, source_basis, receiver_basis, tile_ranks, keep_counts):
    tiles, reps = lax.axis_size("tile"), lax.axis_size("rep")
    _, ranks, _, span = source_basis.shape
    points = focusing.shape[1]
    share = points // reps
    factor = 1.0 / math.sqrt(SPAN * span * tiles)
    reduce_here = (2 * share) % (16 * tiles) == 0
    chunk = 2 * share // tiles if reduce_here else 16
    near = (tiles, ranks, 2 * points) if reduce_here else (1, 16, 128)
    bf = jnp.bfloat16
    dma = pltpu.SemaphoreType.DMA
    smem = pl.BlockSpec(memory_space=pltpu.SMEM)
    vmem = pl.BlockSpec(memory_space=pltpu.VMEM)
    fwd, mar, cor = pl.pallas_call(
        functools.partial(kernel, tiles, reps, reduce_here, factor),
        out_shape=(
            jax.ShapeDtypeStruct((2, share, span), jnp.float32),
            jax.ShapeDtypeStruct((2, share, span), jnp.float32),
            jax.ShapeDtypeStruct((2, share, points), jnp.float32),
        ),
        in_specs=[vmem, vmem, vmem, smem, smem],
        out_specs=(vmem, vmem, vmem),
        scratch_shapes=[
            pltpu.VMEM((2, tiles, ranks, span), bf),
            pltpu.VMEM((2, tiles, ranks, span), bf),
            pltpu.VMEM((reps, 2, tiles, ranks, span), bf),
            pltpu.VMEM((reps, 2, tiles, ranks, span), bf),
            pltpu.VMEM((reps, tiles, ranks, 2 * share), bf),
            pltpu.VMEM((reps, tiles, ranks, 2 * share), bf),
            pltpu.VMEM((reps, tiles, ranks, 2 * share), bf),
            pltpu.VMEM((reps, tiles, ranks, 2 * share), bf),
            pltpu.VMEM((tiles, chunk, points), bf),
            pltpu.VMEM((tiles, chunk, points), bf),
            pltpu.VMEM((tiles, chunk, points), bf),
            pltpu.VMEM(near, bf),
            pltpu.VMEM(near, bf),
            pltpu.VMEM((reps,) + near, bf),
            dma((tiles,)), dma((tiles,)), dma((reps,)), dma((reps,)),
            dma((tiles * reps,)), dma((tiles * reps,)),
            dma((reps,)), dma((reps,)), dma((reps,)), dma((reps,)),
            dma((tiles,)), dma((tiles,)), dma((tiles,)), dma((tiles,)), dma((tiles,)), dma((tiles,)),
        ],
        compiler_params=pltpu.CompilerParams(
            collective_id=0, has_side_effects=True, vmem_limit_bytes=56 * 2 ** 20),
    )(focusing, source_basis, receiver_basis, tile_ranks.reshape(tiles), keep_counts)
    if not reduce_here:
        cor = lax.psum(cor, "tile")
    return fwd, mar, cor


def solution(mesh):
    placed = (
        P(None, "grp", "tile"),
        P(None, "rep", "grp", "tile"),
        P(None, "rep", "grp", "tile"),
        P("grp", "tile"),
        P(("grp", "tile")),
    )
    return jax.shard_map(
        per_device,
        mesh=mesh,
        in_specs=placed,
        out_specs=(
            P(None, ("grp", "rep"), "tile"),
            P(None, ("grp", "rep"), "tile"),
            P(None, "rep", "grp"),
        ),
        check_vma=False,
    )
```

```python
import functools
import math

import jax
import jax.numpy as jnp
from jax import lax
from jax.experimental import pallas as pl
from jax.experimental.pallas import tpu as pltpu
from jax.sharding import PartitionSpec as P

SPAN = 256
BUCKET = 16
FOC = 256
MESH = pl.DeviceIdType.MESH

NT = (((1,), (1,)), ((), ()))
TN = (((0,), (0,)), ((), ()))


def dot(a, b, dims):
    return lax.dot_general(a, b, dims, preferred_element_type=jnp.float32)


def each(first, last, body):
    if last - first <= 16:
        for i in range(first, last):
            body(i)
    else:
        pl.loop(first, last)(body)


def kernel(tiles, reps, reduce_here, factor, foc_hbm, source_hbm, receiver_hbm, ranks_ref, keep_ref,
           fwd_ref, mar_ref, cor_ref,
           foc_ref, source_ref, receiver_ref, load_sem, sb_ref, rb_ref, rb_all, sb_all, coef_out, coef_in, back_out, back_in, red_out, red_in, cor_all,
           near_out, near_in, near_all,
           near_send, near_recv, row_send, row_recv,
           coef_send, coef_recv, rb_send, rb_recv, sb_send, sb_recv,
           back_send, back_recv, red_send, red_recv, cor_send, cor_recv):
    t = lax.axis_index("tile")
    r = lax.axis_index("rep")
    me = t * reps + r
    count = tiles * reps
    loads = [pltpu.make_async_copy(src, dst, load_sem.at[i]) for i, (src, dst) in enumerate(
        [(source_hbm, source_ref), (foc_hbm, foc_ref), (receiver_hbm, receiver_ref)])]
    ranks, span = sb_ref.shape[2], sb_ref.shape[3]
    share = foc_ref.shape[1] // reps
    rows = reps * tiles * ranks

    def peer(d):
        other = lax.rem(me + d, count)
        return other // reps, lax.rem(other, reps)

    for c in loads:
        c.start()
    barrier = pltpu.get_barrier_semaphore()

    def greet(d):
        pt, pr = peer(d)
        pl.semaphore_signal(barrier, inc=1, device_id={"tile": pt, "rep": pr}, device_id_type=MESH)

    each(1, count, greet)

    for c in loads:
        c.wait()
    bucket = (r * ranks + lax.broadcasted_iota(jnp.int32, (2, ranks, span), 1)) // BUCKET
    for a in range(tiles):
        wide = source_ref[:, :, a, :].astype(jnp.float32)
        sb_ref[:, a] = jnp.where(bucket < ranks_ref[a], wide, 0.0).astype(jnp.bfloat16)
        rb_ref[:, a] = receiver_ref[:, :, a, :]

    shares, turned = [], []
    for j in range(reps):
        re = foc_ref[0, j * share:(j + 1) * share, :]
        im = foc_ref[1, j * share:(j + 1) * share, :]
        shares += [re, im]
        turned += [-im, re]
    coef = dot(sb_ref[0].reshape(tiles * ranks, span), jnp.concatenate(shares, 0), NT)
    coef += dot(sb_ref[1].reshape(tiles * ranks, span), jnp.concatenate(turned, 0), NT)
    coef = coef.astype(jnp.bfloat16).reshape(tiles, ranks, reps * 2 * share)
    for j in range(reps):
        coef_out[j] = coef[:, :, j * 2 * share:(j + 1) * 2 * share]

    pl.semaphore_wait(barrier, count - 1)

    class Gather:
        def __init__(self, own, held, send, recv):
            self.own, self.held, self.send, self.recv = own, held, send, recv
            if reps == 4:
                self.first = [self.copy(own, r, r ^ 2, 0), self.copy(own, r, r ^ 1, 1)]
                self.second = [self.copy(held.at[r ^ 2], r ^ 2, r ^ 1, 2)]
            else:
                self.first = [self.copy(own, r, lax.rem(r + d, reps), d - 1) for d in range(1, reps)]
                self.second = []

        def copy(self, src, slot, to, i):
            return pltpu.make_async_remote_copy(
                src_ref=src, dst_ref=self.held.at[slot], send_sem=self.send.at[i], recv_sem=self.recv.at[i],
                device_id={"tile": t, "rep": to}, device_id_type=MESH)

        def start(self):
            for c in self.first:
                c.start()
            self.held[r] = self.own[...]

        def forward(self):
            if self.second:
                self.first[0].wait_recv()
                self.second[0].start()

        def wait_recv(self):
            for c in (self.first[1:] if self.second else self.first) + self.second:
                c.wait_recv()

        def wait_send(self):
            for c in self.first + self.second:
                c.wait_send()

    def coef_copy(d):
        pt, pr = peer(d)
        return pltpu.make_async_remote_copy(
            src_ref=coef_out.at[pr, pt], dst_ref=coef_in.at[r, t],
            send_sem=coef_send.at[d], recv_sem=coef_recv.at[d],
            device_id={"tile": pt, "rep": pr}, device_id_type=MESH)

    def tile_copy(src, dst, send, recv, d):
        return pltpu.make_async_remote_copy(
            src_ref=src, dst_ref=dst, send_sem=send.at[d], recv_sem=recv.at[d],
            device_id={"tile": lax.rem(t + d, tiles), "rep": r}, device_id_type=MESH)

    def near_copy(d):
        return tile_copy(near_out.at[lax.rem(t + d, tiles)], near_in.at[t], near_send, near_recv, d)

    rb_gather = Gather(rb_ref, rb_all, rb_send, rb_recv)
    sb_gather = Gather(sb_ref, sb_all, sb_send, sb_recv)
    row_gather = Gather(near_in, near_all, row_send, row_recv)
    rb_gather.start()
    each(1, count, lambda d: coef_copy(d).start())
    coef_in[r, t] = coef_out[r, t]
    if reduce_here:
        fre, fim = foc_ref[0], foc_ref[1]
        coef = dot(sb_ref[0].reshape(tiles * ranks, span), jnp.concatenate([fre, fim], 0), NT)
        coef += dot(sb_ref[1].reshape(tiles * ranks, span), jnp.concatenate([-fim, fre], 0), NT)
        near_out[...] = coef.astype(jnp.bfloat16).reshape(near_out.shape)
        each(1, tiles, lambda d: near_copy(d).start())
        near_in[t] = near_out[t]

    rb_gather.forward()
    if reduce_here:
        each(1, tiles, lambda d: near_copy(d).wait_recv())
        row_gather.start()
    sb_gather.start()
    rb_gather.wait_recv()
    each(1, count, lambda d: coef_copy(d).wait_recv())

    arrived = coef_in[...].reshape(rows, 2 * share)
    rre = rb_all[:, 0].reshape(rows, span)
    rim = rb_all[:, 1].reshape(rows, span)
    g0 = dot(arrived, rre, TN)
    g1 = dot(arrived, rim, TN)
    fre = g0[:share] - g1[share:]
    fim = g0[share:] + g1[:share]
    fwd_ref[0] = g0.reshape(2, share, span)
    fwd_ref[1, 0] = -g1[share:]
    fwd_ref[1, 1] = g1[:share]
    if reduce_here:
        row_gather.forward()
    kept = lax.broadcasted_iota(jnp.int32, (share, span), 1) < keep_ref[0]
    mre = jnp.where(kept, fre, 0.0).astype(jnp.bfloat16)
    mim = jnp.where(kept, fim, 0.0).astype(jnp.bfloat16)
    back = dot(rre, jnp.concatenate([mre, mim], 0), NT)
    back += dot(rim, jnp.concatenate([mim, -mre], 0), NT)
    back = back.astype(jnp.bfloat16)
    back_out[...] = back.reshape(reps, tiles, ranks, 2 * share)

    def back_copy(d):
        return tile_copy(back_out.at[:, lax.rem(t + d, tiles)], back_in.at[:, t], back_send, back_recv, d)

    def red_copy(d):
        return tile_copy(red_out.at[lax.rem(t + d, tiles)], red_in.at[t], red_send, red_recv, d)

    def cor_copy(d):
        return tile_copy(cor_all.at[t], cor_all.at[t], cor_send, cor_recv, d)

    each(1, tiles, lambda d: back_copy(d).start())
    back_in[:, t] = back_out[:, t]

    if reduce_here:
        row_gather.wait_recv()
        both = dot(back, near_all[...].reshape(rows, 2 * reps * share), TN)
        points = reps * share
        part_re = both[:share, :points] + both[share:, points:]
        part_im = both[share:, :points] - both[:share, points:]
        part = jnp.concatenate([part_re, part_im], 0).astype(jnp.bfloat16)
        red_out[...] = part.reshape(red_out.shape)
        each(1, tiles, lambda d: red_copy(d).start())
        red_in[t] = red_out[t]

    if reduce_here:
        each(1, tiles, lambda d: red_copy(d).wait_recv())
        total = red_in[0].astype(jnp.float32)
        for j in range(1, tiles):
            total += red_in[j].astype(jnp.float32)
        cor_all[t] = total.astype(jnp.bfloat16)
        each(1, tiles, lambda d: cor_copy(d).start())

    sb_gather.forward()
    each(1, tiles, lambda d: back_copy(d).wait_recv())
    sb_gather.wait_recv()
    arrived = back_in[...].reshape(rows, 2 * share)
    h0 = dot(arrived, sb_all[:, 0].reshape(rows, span), TN)
    h1 = dot(arrived, sb_all[:, 1].reshape(rows, span), TN)
    are = h0[:share] + h1[share:]
    aim = h0[share:] - h1[:share]
    mar_ref[0] = h0.reshape(2, share, span)
    mar_ref[1, 0] = h1[share:]
    mar_ref[1, 1] = -h1[:share]

    if reduce_here:
        each(1, count, lambda d: coef_copy(d).wait_send())
        each(1, tiles, lambda d: near_copy(d).wait_send())
        each(1, tiles, lambda d: red_copy(d).wait_send())
        row_gather.wait_send()
        each(1, tiles, lambda d: cor_copy(d).wait_recv())
        cor_ref[...] = cor_all[...].reshape(cor_ref.shape)
        each(1, tiles, lambda d: cor_copy(d).wait_send())
    else:
        are = are.astype(jnp.bfloat16)
        aim = aim.astype(jnp.bfloat16)
        cor_ref[0] = (dot(are, foc_ref[0], NT) + dot(aim, foc_ref[1], NT))
        cor_ref[1] = (dot(aim, foc_ref[0], NT) - dot(are, foc_ref[1], NT))
        each(1, count, lambda d: coef_copy(d).wait_send())
    rb_gather.wait_send()
    sb_gather.wait_send()
    each(1, tiles, lambda d: back_copy(d).wait_send())


def per_device(focusing, source_basis, receiver_basis, tile_ranks, keep_counts):
    tiles, reps = lax.axis_size("tile"), lax.axis_size("rep")
    _, ranks, _, span = source_basis.shape
    points = focusing.shape[1]
    share = points // reps
    factor = 1.0 / math.sqrt(SPAN * span * tiles)
    reduce_here = (2 * share) % (16 * tiles) == 0
    chunk = 2 * share // tiles if reduce_here else 16
    near = (tiles, ranks, 2 * points) if reduce_here else (1, 16, 128)
    bf = jnp.bfloat16
    dma = pltpu.SemaphoreType.DMA
    anywhere = pl.BlockSpec(memory_space=pl.ANY)
    smem = pl.BlockSpec(memory_space=pltpu.SMEM)
    vmem = pl.BlockSpec(memory_space=pltpu.VMEM)
    fwd, mar, cor = pl.pallas_call(
        functools.partial(kernel, tiles, reps, reduce_here, factor),
        out_shape=(
            jax.ShapeDtypeStruct((2, 2, share, span), jnp.float32),
            jax.ShapeDtypeStruct((2, 2, share, span), jnp.float32),
            jax.ShapeDtypeStruct((2, share, points), bf if reduce_here else jnp.float32),
        ),
        in_specs=[anywhere, anywhere, anywhere, smem, smem],
        out_specs=(vmem, vmem, vmem),
        scratch_shapes=[
            pltpu.VMEM(focusing.shape, bf),
            pltpu.VMEM(source_basis.shape, bf),
            pltpu.VMEM(receiver_basis.shape, bf),
            dma((3,)),
            pltpu.VMEM((2, tiles, ranks, span), bf),
            pltpu.VMEM((2, tiles, ranks, span), bf),
            pltpu.VMEM((reps, 2, tiles, ranks, span), bf),
            pltpu.VMEM((reps, 2, tiles, ranks, span), bf),
            pltpu.VMEM((reps, tiles, ranks, 2 * share), bf),
            pltpu.VMEM((reps, tiles, ranks, 2 * share), bf),
            pltpu.VMEM((reps, tiles, ranks, 2 * share), bf),
            pltpu.VMEM((reps, tiles, ranks, 2 * share), bf),
            pltpu.VMEM((tiles, chunk, points), bf),
            pltpu.VMEM((tiles, chunk, points), bf),
            pltpu.VMEM((tiles, chunk, points), bf),
            pltpu.VMEM(near, bf),
            pltpu.VMEM(near, bf),
            pltpu.VMEM((reps,) + near, bf),
            dma((tiles,)), dma((tiles,)), dma((reps,)), dma((reps,)),
            dma((tiles * reps,)), dma((tiles * reps,)),
            dma((reps,)), dma((reps,)), dma((reps,)), dma((reps,)),
            dma((tiles,)), dma((tiles,)), dma((tiles,)), dma((tiles,)), dma((tiles,)), dma((tiles,)),
        ],
        compiler_params=pltpu.CompilerParams(
            collective_id=0, has_side_effects=True, vmem_limit_bytes=56 * 2 ** 20),
    )(focusing, source_basis, receiver_basis, tile_ranks.reshape(tiles), keep_counts)
    if not reduce_here:
        cor = lax.psum(cor, "tile")
    return fwd[0] + fwd[1], mar[0] + mar[1], factor * cor.astype(jnp.float32)


def solution(mesh):
    placed = (
        P(None, "grp", "tile"),
        P(None, "rep", "grp", "tile"),
        P(None, "rep", "grp", "tile"),
        P("grp", "tile"),
        P(("grp", "tile")),
    )
    return jax.shard_map(
        per_device,
        mesh=mesh,
        in_specs=placed,
        out_specs=(
            P(None, ("grp", "rep"), "tile"),
            P(None, ("grp", "rep"), "tile"),
            P(None, "rep", "grp"),
        ),
        check_vma=False,
    )
```
